32 devices in a mesh: seg: 4 (over y, x), dir: 8 (over z, core).
Axes of the slice: x: 2, y: 2, z: 4, core: 2. Of those that a mesh axis runs over, the one named last changes fastest.
Arguments:
- panel: bfloat16 [16, 45056], P('dir'), may hold values from -6 to 6
- seeds: bfloat16 [4, 16, 45056], P('seg', 'dir'), may hold values from -6 to 6
- inverses: bfloat16 [4, 352, 128, 128], P('seg', 'dir'), may hold values from -1 to 1
- coupling: bfloat16 [4, 3, 128, 128], P('seg'), may hold values from -0.5 to 0.5
- weights: float32 [352, 3], replicated, may hold values from -0.3 to 0.3
- pattern: int32 [352, 3], replicated, may hold values from 0 to 351
- counts: int32 [4], replicated, may hold values from 1 to 2, as said below
Outputs:
- tangent: bfloat16 [4, 16, 45056], P('seg', 'dir')
- adjoint: bfloat16 [4, 16, 45056], P('seg', 'dir')
- projected: float32 [16, 16], P('dir')
The draws below stay inside these ranges and needn't reach their ends.
Inputs may be any that keep to these rules, and one draw needn't show every extreme that they name: `counts`: some segment takes 2 time steps.
All inputs are finite; a program needn't handle non-finite values.
Results may differ from the reference program's by a relative error of at most 0.019.
Values may be sent and summed in bfloat16 or wider, within the bound.
A program may use at most 64 MiB of HBM per device.

```python
import math
import jax
import jax.numpy as jnp

NB = 352
BLOCK = 128
COUPLE = 3
STEPS_MAX = 2
DIRS = 16
SEGS = 4
NS = 45056


def draw_inverses(key, part):
    diag_key, off_key = jax.random.split(jax.random.fold_in(key, 17))
    diagonal = jax.random.uniform(diag_key, (SEGS, NB, BLOCK), jnp.float32, 0.7, 0.88)
    spread = 0.35
    off_part = jax.random.uniform(off_key, (SEGS, NB, BLOCK, BLOCK), jnp.float32, -1.0, 1.0) * (spread * BLOCK ** (-0.5))
    identity = jnp.eye(BLOCK, dtype=jnp.float32)
    return (off_part + diagonal[..., None] * identity).astype(jnp.bfloat16)


def draw_counts(key, part):
    first_key, second_key = jax.random.split(jax.random.fold_in(key, 23))
    steps_drawn = jax.random.randint(first_key, (SEGS,), 1, STEPS_MAX + 1)
    longest = jax.random.randint(second_key, (), 0, SEGS)
    return steps_drawn.at[longest].set(STEPS_MAX).astype(jnp.int32)


def set_ends(drawn, stream_key, smallest, top_value):
    spot = [jax.random.randint(jax.random.fold_in(stream_key, axis), (), 0, length) for axis, length in enumerate(drawn.shape)]
    main_axis = drawn.shape.index(max(drawn.shape))
    neighbour = spot[:main_axis] + [(spot[main_axis] + 1) % drawn.shape[main_axis]] + spot[main_axis + 1:]
    return drawn.at[tuple(spot)].set(smallest).at[tuple(neighbour)].set(top_value)


def shard_levels(stream_key, extent, cuts, least, top_value):
    factor_of = 1.0
    for dim, shards_of in cuts:
        steps = jax.random.uniform(jax.random.fold_in(jax.random.fold_in(stream_key, 6), dim), (shards_of,), jnp.float32, least / len(cuts), top_value / len(cuts))
        factor_of = factor_of * jnp.repeat(jnp.exp(steps), extent[dim] // shards_of).reshape((-1,) + (1,) * (len(extent) - 1 - dim))
    return factor_of


def noise(stream_key, dims, deviation, reach, pieces=(), kind=jnp.bfloat16):
    factor_of = shard_levels(stream_key, dims, pieces, -0.22, 0.18) if pieces else 1.0
    result = jax.random.normal(stream_key, dims, jnp.float32) * deviation * factor_of
    return jnp.minimum(jnp.maximum(result, -reach), reach).astype(kind)


def setup_inputs(seed: int = 0) -> dict:
    key_list = jax.random.split(jax.random.key(seed), 8)
    panel = noise(key_list[0], (DIRS, NS), 1.0, 6.0, ((0, 8),))
    seeds = noise(key_list[1], (SEGS, DIRS, NS), 1.0, 6.0, ((0, 4), (1, 8)))
    inverses = draw_inverses(jax.random.fold_in(key_list[7], 71), 0)
    coupling = noise(key_list[3], (SEGS, COUPLE, BLOCK, BLOCK), BLOCK ** -0.5, 0.5, ((0, 4),))
    weights = jnp.clip(jax.random.uniform(key_list[4], (NB, COUPLE), jnp.float32, -0.3, 0.3), -0.3, 0.3)
    pattern = set_ends(jax.random.randint(key_list[5], (NB, COUPLE), 0, NB), jax.random.fold_in(key_list[5], 1), 0, NB - 1).astype(jnp.int32)
    counts = draw_counts(jax.random.fold_in(key_list[7], 71), 0)
    return {"panel": panel, "seeds": seeds, "inverses": inverses, "coupling": coupling, "weights": weights, "pattern": pattern, "counts": counts}


def step_forward(current, inverse_table, coupling, weights, pattern):
    picked = current[:, pattern, :].astype(jnp.float32)
    mixed = (picked * weights[None, :, :, None]).astype(jnp.bfloat16)
    pushed = jnp.einsum('rnkb,keb->rne', mixed.astype(jnp.float32), coupling.astype(jnp.float32))
    forced = (current.astype(jnp.float32) + pushed).astype(jnp.bfloat16)
    return jnp.einsum('ieq,riq->rie', inverse_table.astype(jnp.float32), forced.astype(jnp.float32)).astype(jnp.bfloat16)

def step_adjoint(current, inverse_table, coupling, weights, pattern):
    reached = jnp.einsum('ieq,rie->riq', inverse_table.astype(jnp.float32), current.astype(jnp.float32)).astype(jnp.bfloat16)
    pulled = jnp.einsum('rne,keb->rnkb', reached.astype(jnp.float32), coupling.astype(jnp.float32)).astype(jnp.bfloat16)
    terms = pulled.astype(jnp.float32) * weights[None, :, :, None]
    spread = jnp.zeros(reached.shape, jnp.float32).at[:, pattern, :].add(terms)
    return (reached.astype(jnp.float32) + spread).astype(jnp.bfloat16)

def reference(panel, seeds, inverses, coupling, weights, pattern, counts):
    current = panel.reshape(DIRS, NB, BLOCK)
    tangents = []
    for segment in range(SEGS):
        for step_index in range(STEPS_MAX):
            advanced = step_forward(current, inverses[segment], coupling[segment], weights, pattern)
            current = jnp.where(step_index < counts[segment], advanced, current)
        tangents.append(current)
    adjoints = [None] * SEGS
    carried = jnp.zeros((DIRS, NB, BLOCK), jnp.bfloat16)
    order_list = [(1 - round_index) % SEGS for round_index in range(SEGS)]
    for segment in order_list:
        current = (seeds[segment].reshape(DIRS, NB, BLOCK).astype(jnp.float32) + carried.astype(jnp.float32)).astype(jnp.bfloat16)
        for step_index in range(STEPS_MAX):
            advanced = step_adjoint(current, inverses[segment], coupling[segment], weights, pattern)
            current = jnp.where(step_index < counts[segment], advanced, current)
        adjoints[segment] = current
        carried = current
    projected = jnp.zeros((DIRS, DIRS), jnp.float32)
    for segment in range(SEGS):
        left_panel = adjoints[segment].reshape(DIRS, NS)
        right_panel = tangents[segment].reshape(DIRS, NS)
        projected = projected + jnp.dot(left_panel, right_panel.T, preferred_element_type=jnp.float32)
    projected = projected * (1.0 / math.sqrt(NS * SEGS))
    tangent = jnp.stack([item.reshape(DIRS, NS) for item in tangents])
    adjoint = jnp.stack([item.reshape(DIRS, NS) for item in adjoints])
    return (tangent, adjoint, projected)
```

```python
import functools
import math

import jax
import jax.numpy as jnp
from jax import lax
from jax.experimental import pallas as pl
from jax.experimental.pallas import tpu as pltpu
from jax.sharding import PartitionSpec as P

MESH = pl.DeviceIdType.MESH
F32 = jnp.float32
BF16 = jnp.bfloat16

SEED, F1, F2, F3, TAN, HAND_F, HAND_G, G2, G3, G4, ADJ = range(11)
EXCHANGES = 11


def kernel(
    dims,
    panel_ref, seeds_ref, inv_ref, cf_ref, cg_ref, wf_ref, wg_ref, counts_ref,
    tangent_ref, adjoint_ref, proj_ref,
    land, f1s, f2s, f3s, tans, g2s, g3s, g4s, adjs, ubuf, obuf, pbuf, rp, qbuf, rq,
    send_sem, recv_sem, ps_sem, pr_sem, qs_sem, qr_sem,
):
    S, D, R, nb, pb, B, K, scale = dims
    N = D * pb
    rows = D * R
    s = lax.axis_index("seg")
    d = lax.axis_index("dir")

    barrier = pltpu.get_barrier_semaphore()
    total = S * D
    lin = s * D + d

    def greet(o, c):
        t = lax.rem(lin + o, total)
        pl.semaphore_signal(
            barrier, inc=1, device_id=(lax.div(t, D), lax.rem(t, D)), device_id_type=MESH
        )
        return c

    lax.fori_loop(1, total, greet, 0)
    pl.semaphore_wait(barrier, total - 1)

    ubuf[...] = jnp.zeros_like(ubuf)
    obuf[...] = jnp.zeros_like(obuf)

    def copy(src, ex, seg, to, came_from):
        return pltpu.make_async_remote_copy(
            src_ref=src.at[to],
            dst_ref=land.at[ex, came_from],
            send_sem=send_sem.at[ex, to],
            recv_sem=recv_sem.at[ex, came_from],
            device_id=(seg, to),
            device_id_type=MESH,
        )

    def send_group(src, ex):
        def one(o, c):
            copy(src, ex, s, lax.rem(d + o, D), d).start()
            return c

        lax.fori_loop(1, D, one, 0)
        land[ex, d] = src[d]

    def wait_group(src, ex):
        def one(o, c):
            j = lax.rem(d + D - o, D)
            copy(src, ex, s, j, j).wait_recv()
            return c

        lax.fori_loop(1, D, one, 0)

    def sent_group(src, ex):
        def one(o, c):
            copy(src, ex, s, lax.rem(d + o, D), d).wait_send()
            return c

        lax.fori_loop(1, D, one, 0)

    def send_on(src, ex, seg):
        def one(o, c):
            copy(src, ex, seg, lax.rem(d + o, D), d).start()
            return c

        lax.fori_loop(0, D, one, 0)

    def wait_on(src, ex, seg):
        def one(o, c):
            copy(src, ex, seg, o, o).wait_recv()
            return c

        lax.fori_loop(0, D, one, 0)

    def sent_on(src, ex, seg):
        def one(o, c):
            copy(src, ex, seg, o, d).wait_send()
            return c

        lax.fori_loop(0, D, one, 0)

    def couple(x, w_ref, c_ref):
        parts = [jnp.dot(v, c_ref[...], preferred_element_type=F32).astype(BF16) for v in x]
        rhs = jnp.concatenate(
            [
                jnp.concatenate([p[:, k * B : (k + 1) * B] for p in parts], axis=1)
                for k in range(K)
            ],
            axis=0,
        )
        acc = jnp.dot(w_ref[...], rhs, preferred_element_type=F32)
        return [x[r].astype(F32) + acc[:, r * B : (r + 1) * B] for r in range(R)]

    def split(value):
        return [value[:, r].reshape(N, B) for r in range(R)]

    def put(ref, parts):
        for r in range(R):
            ref[:, r] = parts[r].astype(BF16).reshape(D, pb, B)

    group = max(g for g in range(1, 17) if nb % g == 0)

    def invert(value, contract):
        ubuf[...] = value.astype(F32).reshape(rows * pb, B)

        def step(g, c):
            for u in range(group):
                at = pl.ds(g * group + u, rows, stride=pb)
                obuf[at, :] = lax.dot_general(
                    ubuf[at, :].astype(BF16),
                    inv_ref[g * group + u],
                    (((1,), (contract,)), ((), ())),
                    preferred_element_type=F32,
                )
            return c

        lax.fori_loop(0, nb // group, step, 0)
        return obuf[...].astype(BF16).reshape(D, R, pb, B)

    send_group(seeds_ref, SEED)
    more = counts_ref[s] > 1

    def tangent_round():
        @pl.when(s > 0)
        def _():
            wait_on(tans, HAND_F, s)

        first = jnp.where(s > 0, land[HAND_F], panel_ref[...])
        put(f1s, couple(split(first), wf_ref, cf_ref))
        send_group(f1s, F1)
        wait_group(f1s, F1)
        f2s[...] = invert(land[F1], 1)
        send_group(f2s, F2)
        wait_group(f2s, F2)
        put(f3s, couple(split(land[F2]), wf_ref, cf_ref))
        send_group(f3s, F3)
        wait_group(f3s, F3)
        tans[...] = jnp.where(more, invert(land[F3], 1), f2s[...])

        @pl.when(s < S - 1)
        def _():
            send_on(tans, HAND_F, lax.rem(s + 1, S))

        send_group(tans, TAN)

    def adjoint_round():
        wait_group(seeds_ref, SEED)

        @pl.when(s != 1)
        def _():
            wait_on(adjs, HAND_G, s)

        entry = jnp.where(
            s != 1,
            (land[SEED].astype(F32) + land[HAND_G].astype(F32)).astype(BF16),
            land[SEED],
        )
        g2s[...] = invert(entry, 0)
        send_group(g2s, G2)
        wait_group(g2s, G2)
        put(g3s, couple(split(land[G2]), wg_ref, cg_ref))
        send_group(g3s, G3)
        wait_group(g3s, G3)
        g4s[...] = invert(land[G3], 0)
        send_group(g4s, G4)
        wait_group(g4s, G4)
        done = couple(split(land[G4]), wg_ref, cg_ref)
        put(adjs, done)
        adjs[...] = jnp.where(more, adjs[...], g3s[...])

        @pl.when(s != 2)
        def _():
            send_on(adjs, HAND_G, lax.rem(s + S - 1, S))

        send_group(adjs, ADJ)

    tangent_first = s < lax.rem(1 - s + S, S)

    def turn(slot, c):
        now = (slot == 0) == tangent_first

        @pl.when(now)
        def _():
            tangent_round()

        @pl.when(jnp.logical_not(now))
        def _():
            adjoint_round()

        return c

    lax.fori_loop(0, 2, turn, 0)

    adjoint_ref[...] = adjs[...]
    wait_group(adjs, ADJ)
    ubuf[...] = land[ADJ].astype(F32).reshape(rows * pb, B)
    obuf[...] = tans[...].astype(F32).reshape(rows * pb, B)

    def gram(g, acc):
        spots = [pl.ds(g * group + u, rows, stride=pb) for u in range(group)]
        left = jnp.concatenate([ubuf[at, :].astype(BF16) for at in spots], axis=1)
        right = jnp.concatenate([obuf[at, :].astype(BF16) for at in spots], axis=1)
        return acc + lax.dot_general(
            left, right, (((1,), (1,)), ((), ())), preferred_element_type=F32
        )

    pbuf[...] = jnp.zeros_like(pbuf)
    pbuf[:, 0:rows] = lax.fori_loop(0, nb // group, gram, jnp.zeros((rows, rows), F32))

    def pcopy(to, came_from):
        return pltpu.make_async_remote_copy(
            src_ref=pbuf, dst_ref=rp.at[came_from], send_sem=ps_sem.at[to],
            recv_sem=pr_sem.at[came_from], device_id=(s, to), device_id_type=MESH,
        )

    def qcopy(to, came_from):
        return pltpu.make_async_remote_copy(
            src_ref=qbuf, dst_ref=rq.at[came_from], send_sem=qs_sem.at[to],
            recv_sem=qr_sem.at[came_from], device_id=(to, d), device_id_type=MESH,
        )

    rp[d] = pbuf[...]
    for o in range(1, D):
        pcopy(lax.rem(d + o, D), d).start()
    for o in range(1, D):
        j = lax.rem(d + D - o, D)
        pcopy(j, j).wait_recv()
    qbuf[...] = jnp.sum(rp[...], axis=0)
    rq[s] = qbuf[...]
    for o in range(1, S):
        qcopy(lax.rem(s + o, S), s).start()
    wait_group(tans, TAN)
    tangent_ref[...] = land[TAN]
    for o in range(1, S):
        j = lax.rem(s + S - o, S)
        qcopy(j, j).wait_recv()
    for o in range(1, D):
        pcopy(lax.rem(d + o, D), d).wait_send()
    pbuf[...] = jnp.sum(rq[...], axis=0) * scale
    proj_ref[...] = pbuf[pl.ds(d * R, R), :]

    for o in range(1, S):
        qcopy(lax.rem(s + o, S), s).wait_send()
    for src, ex in (
        (seeds_ref, SEED), (f1s, F1), (f2s, F2), (f3s, F3), (tans, TAN),
        (g2s, G2), (g3s, G3), (g4s, G4), (adjs, ADJ),
    ):
        sent_group(src, ex)

    @pl.when(s < S - 1)
    def _():
        sent_on(tans, HAND_F, lax.rem(s + 1, S))

    @pl.when(s != 2)
    def _():
        sent_on(adjs, HAND_G, lax.rem(s + S - 1, S))


def body(panel, seeds, inverses, coupling, weights, pattern, counts):
    NB, K = pattern.shape
    B = coupling.shape[-1]
    R = panel.shape[0]
    S, D = lax.axis_size("seg"), lax.axis_size("dir")
    nb = NB // D
    pb = -(-nb // 16) * 16
    N = D * pb
    rows = D * R

    def padded(flat):
        cut = flat.reshape(R, D, nb, B).transpose(1, 0, 2, 3)
        return jnp.pad(cut, ((0, 0), (0, 0), (0, pb - nb), (0, 0)))

    def flat(cut):
        return cut[:, :, :nb].transpose(1, 0, 2, 3).reshape(R, NB * B)

    place = (pattern // nb) * pb + pattern % nb
    place = jnp.pad(place.reshape(D, nb, K), ((0, 0), (0, pb - nb), (0, 0)), constant_values=-1)
    place = place.reshape(N, K)
    factor = jnp.pad(weights.reshape(D, nb, K), ((0, 0), (0, pb - nb), (0, 0))).reshape(N, K)
    spot = jnp.arange(N, dtype=jnp.int32)
    wf = jnp.where(
        place[:, :, None] == spot[None, None, :], factor[:, :, None], 0.0
    ).astype(BF16).reshape(N, K * N)
    place_t, factor_t = place.T.reshape(1, K * N), factor.T.reshape(1, K * N)
    wg = jnp.where(place_t == spot[:, None], factor_t, 0.0).astype(BF16)
    cf = coupling[0].transpose(2, 0, 1).reshape(B, K * B)
    cg = coupling[0].transpose(1, 0, 2).reshape(B, K * B)

    dims = (S, D, R, nb, pb, B, K, 1.0 / math.sqrt(NB * B * S))
    panel_buf = (D, R, pb, B)
    vm = pl.BlockSpec(memory_space=pltpu.VMEM)
    tangent, adjoint, proj = pl.pallas_call(
        functools.partial(kernel, dims),
        out_shape=(
            jax.ShapeDtypeStruct(panel_buf, BF16),
            jax.ShapeDtypeStruct(panel_buf, BF16),
            jax.ShapeDtypeStruct((R, 128), F32),
        ),
        in_specs=[vm] * 7 + [pl.BlockSpec(memory_space=pltpu.SMEM)],
        out_specs=(vm, vm, vm),
        scratch_shapes=[pltpu.VMEM((EXCHANGES,) + panel_buf, BF16)]
        + [pltpu.VMEM(panel_buf, BF16)] * 8
        + [
            pltpu.VMEM((rows * pb, B), F32),
            pltpu.VMEM((rows * pb, B), F32),
            pltpu.VMEM((rows, 128), F32),
            pltpu.VMEM((D, rows, 128), F32),
            pltpu.VMEM((rows, 128), F32),
            pltpu.VMEM((S, rows, 128), F32),
            pltpu.SemaphoreType.DMA((EXCHANGES, D)),
            pltpu.SemaphoreType.DMA((EXCHANGES, D)),
            pltpu.SemaphoreType.DMA((D,)),
            pltpu.SemaphoreType.DMA((D,)),
            pltpu.SemaphoreType.DMA((S,)),
            pltpu.SemaphoreType.DMA((S,)),
        ],
        compiler_params=pltpu.CompilerParams(
            collective_id=0, has_side_effects=True, vmem_limit_bytes=48 * 2**20
        ),
    )(padded(panel), padded(seeds[0]), inverses[0], cf, cg, wf, wg, counts)
    return flat(tangent)[None], flat(adjoint)[None], proj[:, :rows]


def solution(mesh):
    in_specs = (
        P("dir", None),
        P("seg", "dir", None),
        P("seg", "dir", None, None),
        P("seg", None, None, None),
        P(),
        P(),
        P(),
    )
    out_specs = (P("seg", "dir", None), P("seg", "dir", None), P("dir", None))
    return jax.shard_map(body, mesh=mesh, in_specs=in_specs, out_specs=out_specs, check_vma=False)
```

```python
import functools
import math

import jax
import jax.numpy as jnp
from jax import lax
from jax.experimental import pallas as pl
from jax.experimental.pallas import tpu as pltpu
from jax.sharding import PartitionSpec as P

MESH = pl.DeviceIdType.MESH
F32 = jnp.float32
BF16 = jnp.bfloat16

SEED, F1, F2, F3, TAN, HAND_F, HAND_G, G2, G3, G4, ADJ = range(11)
EXCHANGES = 11


def kernel(
    dims,
    panel_ref, seeds_ref, inv_ref, coup_ref, pat_ref, wts_ref, counts_ref,
    tangent_ref, adjoint_ref, proj_ref,
    land, f1s, f2s, f3s, tans, g2s, g3s, g4s, adjs, wf, wg, ubuf, obuf, pbuf, rp, qbuf, rq,
    send_sem, recv_sem, ps_sem, pr_sem, qs_sem, qr_sem,
):
    S, D, R, NG, nb, pb, B, K, scale = dims
    RG = R // NG
    N = D * pb
    rows = D * RG
    dirs = D * R
    s = lax.axis_index("seg")
    d = lax.axis_index("dir")
    tangent_first = s < lax.rem(1 - s + S, S)
    groups = range(NG)

    def partner(x):
        if D & (D - 1):
            return lax.rem(d + x, D)
        to, bit = d, 1
        while bit < D:
            if x & bit:
                to = to + bit * (1 - 2 * lax.rem(lax.div(d, bit), 2))
            bit *= 2
        return to

    def source(x):
        return lax.rem(d + D - x, D) if D & (D - 1) else partner(x)

    others = range(D - 1, 0, -1)

    barrier = pltpu.get_barrier_semaphore()
    total = S * D
    lin = s * D + d

    def greet(o, c):
        t = lax.rem(lin + o, total)
        pl.semaphore_signal(
            barrier, inc=1, device_id=(lax.div(t, D), lax.rem(t, D)), device_id_type=MESH
        )
        return c

    lax.fori_loop(1, total, greet, 0)

    spot = lax.broadcasted_iota(jnp.int32, (N, N), 1)

    def forward_matrix():
        for k in range(K):
            wf[:, k * N : (k + 1) * N] = jnp.where(
                pat_ref[:, k : k + 1] == spot, wts_ref[:, k : k + 1], 0.0
            ).astype(BF16)

    def adjoint_matrix():
        for k in range(K):
            wg[:, k * N : (k + 1) * N] = jnp.where(
                pat_ref[:, k : k + 1] == spot, wts_ref[:, k : k + 1], 0.0
            ).T.astype(BF16)

    @pl.when(tangent_first)
    def _():
        forward_matrix()

    obuf[...] = jnp.zeros_like(obuf)
    pl.semaphore_wait(barrier, total - 1)

    def copy(src, ex, g, seg, to, came_from):
        return pltpu.make_async_remote_copy(
            src_ref=src.at[g, to],
            dst_ref=land.at[ex, g, came_from],
            send_sem=send_sem.at[ex, g, to],
            recv_sem=recv_sem.at[ex, g, came_from],
            device_id=(seg, to),
            device_id_type=MESH,
        )

    def send_group(src, ex, g):
        for x in others:
            copy(src, ex, g, s, partner(x), d).start()
        land[ex, g, d] = src[g, d]

    def wait_group(src, ex, g):
        for x in others:
            j = source(x)
            copy(src, ex, g, s, j, j).wait_recv()

    def sent_group(src, ex):
        def one(o, c):
            for g in groups:
                copy(src, ex, g, s, lax.rem(d + o, D), d).wait_send()
            return c

        lax.fori_loop(1, D, one, 0)

    def send_on(src, ex, g, seg):
        for x in list(others) + [0]:
            copy(src, ex, g, seg, partner(x), d).start()

    def wait_on(src, ex, g, seg):
        for j in range(D):
            copy(src, ex, g, seg, j, j).wait_recv()

    def sent_on(src, ex, seg):
        def one(o, c):
            for g in groups:
                copy(src, ex, g, seg, o, d).wait_send()
            return c

        lax.fori_loop(0, D, one, 0)

    def couple(value, w_ref, contract):
        x = [value[:, r].reshape(N, B) for r in range(RG)]
        rhs = jnp.concatenate(
            [
                jnp.concatenate(
                    [
                        lax.dot_general(
                            v, coup_ref[k], (((1,), (contract,)), ((), ())),
                            preferred_element_type=F32,
                        ).astype(BF16)
                        for v in x
                    ],
                    axis=1,
                )
                for k in range(K)
            ],
            axis=0,
        )
        acc = jnp.dot(w_ref[...], rhs, preferred_element_type=F32)
        out = [x[r].astype(F32) + acc[:, r * B : (r + 1) * B] for r in range(RG)]
        return [v.astype(BF16).reshape(D, pb, B) for v in out]

    def put(ref, g, parts):
        for r in range(RG):
            ref[g, :, r] = parts[r]

    batch = max(n for n in range(1, 17) if nb % n == 0)

    def invert(value, contract):
        ubuf[...] = value.astype(F32).reshape(rows * pb, B)

        def step(i, c):
            for u in range(batch):
                at = pl.ds(i * batch + u, rows, stride=pb)
                obuf[at, :] = lax.dot_general(
                    ubuf[at, :].astype(BF16),
                    inv_ref[i * batch + u],
                    (((1,), (contract,)), ((), ())),
                    preferred_element_type=F32,
                )
            return c

        lax.fori_loop(0, nb // batch, step, 0)
        return obuf[...].astype(BF16).reshape(D, RG, pb, B)

    more = counts_ref[s] > 1

    def tangent_round():
        for g in groups:
            @pl.when(s > 0)
            def _():
                wait_on(tans, HAND_F, g, s)

            first = jnp.where(s > 0, land[HAND_F, g], panel_ref[g])
            put(f1s, g, couple(first, wf, 1))
            send_group(f1s, F1, g)

        @pl.when(tangent_first)
        def _():
            for g in groups:
                send_group(seeds_ref, SEED, g)
            adjoint_matrix()

        for g in groups:
            wait_group(f1s, F1, g)
            f2s[g] = invert(land[F1, g], 1)
            send_group(f2s, F2, g)
        for g in groups:
            wait_group(f2s, F2, g)
            put(f3s, g, couple(land[F2, g], wf, 1))
            send_group(f3s, F3, g)
        for g in groups:
            wait_group(f3s, F3, g)
            tans[g] = jnp.where(more, invert(land[F3, g], 1), f2s[g])

            @pl.when(s < S - 1)
            def _():
                send_on(tans, HAND_F, g, lax.rem(s + 1, S))

        for g in groups:
            send_group(tans, TAN, g)

    def adjoint_round():
        @pl.when(jnp.logical_not(tangent_first))
        def _():
            for g in groups:
                send_group(seeds_ref, SEED, g)

        @pl.when(jnp.logical_not(tangent_first))
        def _():
            adjoint_matrix()
            forward_matrix()

        for g in groups:
            wait_group(seeds_ref, SEED, g)

            @pl.when(s != 1)
            def _():
                wait_on(adjs, HAND_G, g, s)

            entry = jnp.where(
                s != 1,
                (land[SEED, g].astype(F32) + land[HAND_G, g].astype(F32)).astype(BF16),
                land[SEED, g],
            )
            g2s[g] = invert(entry, 0)
            send_group(g2s, G2, g)
        for g in groups:
            wait_group(g2s, G2, g)
            put(g3s, g, couple(land[G2, g], wg, 0))
            send_group(g3s, G3, g)
        for g in groups:
            wait_group(g3s, G3, g)
            g4s[g] = invert(land[G3, g], 0)
            send_group(g4s, G4, g)
        for g in groups:
            wait_group(g4s, G4, g)
            last = couple(land[G4, g], wg, 0)
            put(adjs, g, [jnp.where(more, last[r], g3s[g, :, r]) for r in range(RG)])

            @pl.when(s != 2)
            def _():
                send_on(adjs, HAND_G, g, lax.rem(s + S - 1, S))

        for g in groups:
            send_group(adjs, ADJ, g)

    def turn(slot, c):
        now = (slot == 0) == tangent_first

        @pl.when(now)
        def _():
            tangent_round()

        @pl.when(jnp.logical_not(now))
        def _():
            adjoint_round()

        return c

    lax.fori_loop(0, 2, turn, 0)

    for g in groups:
        for r in range(RG):
            adjoint_ref[:, g * RG + r] = adjs[g, :, r]

    pbuf[...] = jnp.zeros_like(pbuf)

    def gathered(buf, i):
        return jnp.concatenate(
            [buf[pl.ds(i * batch + u, rows, stride=pb), :].astype(BF16) for u in range(batch)],
            axis=1,
        )

    for g in groups:
        wait_group(adjs, ADJ, g)
        ubuf[...] = land[ADJ, g].astype(F32).reshape(rows * pb, B)
        for h in groups:
            obuf[...] = tans[h].astype(F32).reshape(rows * pb, B)

            def gram(i, acc):
                return acc + lax.dot_general(
                    gathered(ubuf, i), gathered(obuf, i), (((1,), (1,)), ((), ())),
                    preferred_element_type=F32,
                )

            pbuf[g * rows : (g + 1) * rows, h * rows : (h + 1) * rows] = lax.fori_loop(
                0, nb // batch, gram, jnp.zeros((rows, rows), F32)
            )

    def pcopy(to, came_from):
        return pltpu.make_async_remote_copy(
            src_ref=pbuf, dst_ref=rp.at[came_from], send_sem=ps_sem.at[to],
            recv_sem=pr_sem.at[came_from], device_id=(s, to), device_id_type=MESH,
        )

    def qcopy(to, came_from):
        return pltpu.make_async_remote_copy(
            src_ref=qbuf, dst_ref=rq.at[came_from], send_sem=qs_sem.at[to],
            recv_sem=qr_sem.at[came_from], device_id=(to, d), device_id_type=MESH,
        )

    for x in others:
        pcopy(partner(x), d).start()
    rp[d] = pbuf[...]
    for x in others:
        j = source(x)
        pcopy(j, j).wait_recv()
    qbuf[...] = jnp.sum(rp[...], axis=0)
    for o in range(1, S):
        qcopy(lax.rem(s + o, S), s).start()
    rq[s] = qbuf[...]
    for g in groups:
        wait_group(tans, TAN, g)
        for r in range(RG):
            tangent_ref[:, g * RG + r] = land[TAN, g, :, r]
    for x in others:
        pcopy(partner(x), d).wait_send()
    for src, ex in (
        (seeds_ref, SEED), (f1s, F1), (f2s, F2), (f3s, F3), (tans, TAN),
        (g2s, G2), (g3s, G3), (g4s, G4), (adjs, ADJ),
    ):
        sent_group(src, ex)

    @pl.when(s < S - 1)
    def _():
        sent_on(tans, HAND_F, lax.rem(s + 1, S))

    @pl.when(s != 2)
    def _():
        sent_on(adjs, HAND_G, lax.rem(s + S - 1, S))

    for o in range(1, S):
        j = lax.rem(s + S - o, S)
        qcopy(j, j).wait_recv()
    pbuf[...] = jnp.sum(rq[...], axis=0) * scale
    for g in groups:
        proj_ref[g * RG : (g + 1) * RG, :] = pbuf[pl.ds(g * rows + d * RG, RG), :]
    for o in range(1, S):
        qcopy(lax.rem(s + o, S), s).wait_send()


def body(panel, seeds, inverses, coupling, weights, pattern, counts):
    NB, K = pattern.shape
    B = coupling.shape[-1]
    R = panel.shape[0]
    S, D = lax.axis_size("seg"), lax.axis_size("dir")
    nb = NB // D
    pb = -(-nb // 16) * 16
    N = D * pb
    NG = 2 if R % 2 == 0 else 1
    RG = R // NG
    rows, dirs = D * RG, D * R

    def padded(flat):
        cut = flat.reshape(NG, RG, D, nb, B).transpose(0, 2, 1, 3, 4)
        return jnp.pad(cut, ((0, 0),) * 3 + ((0, pb - nb), (0, 0)))

    def flat(cut):
        return cut[:, :, :nb].transpose(1, 0, 2, 3).reshape(R, NB * B)

    place = (pattern // nb) * pb + pattern % nb
    gap = ((0, 0), (0, pb - nb), (0, 0))
    place = jnp.pad(place.reshape(D, nb, K), gap, constant_values=-1).reshape(N, K)
    factor = jnp.pad(weights.reshape(D, nb, K), gap).reshape(N, K)

    dims = (S, D, R, NG, nb, pb, B, K, 1.0 / math.sqrt(NB * B * S))
    panel_buf = (NG, D, RG, pb, B)
    vm = pl.BlockSpec(memory_space=pltpu.VMEM)
    tangent, adjoint, proj = pl.pallas_call(
        functools.partial(kernel, dims),
        out_shape=(
            jax.ShapeDtypeStruct((D, R, pb, B), BF16),
            jax.ShapeDtypeStruct((D, R, pb, B), BF16),
            jax.ShapeDtypeStruct((R, 128), F32),
        ),
        in_specs=[vm] * 6 + [pl.BlockSpec(memory_space=pltpu.SMEM)],
        out_specs=(vm, vm, vm),
        scratch_shapes=[pltpu.VMEM((EXCHANGES,) + panel_buf, BF16)]
        + [pltpu.VMEM(panel_buf, BF16)] * 8
        + [
            pltpu.VMEM((N, K * N), BF16),
            pltpu.VMEM((N, K * N), BF16),
            pltpu.VMEM((rows * pb, B), F32),
            pltpu.VMEM((rows * pb, B), F32),
            pltpu.VMEM((dirs, 128), F32),
            pltpu.VMEM((D, dirs, 128), F32),
            pltpu.VMEM((dirs, 128), F32),
            pltpu.VMEM((S, dirs, 128), F32),
            pltpu.SemaphoreType.DMA((EXCHANGES, NG, D)),
            pltpu.SemaphoreType.DMA((EXCHANGES, NG, D)),
            pltpu.SemaphoreType.DMA((D,)),
            pltpu.SemaphoreType.DMA((D,)),
            pltpu.SemaphoreType.DMA((S,)),
            pltpu.SemaphoreType.DMA((S,)),
        ],
        compiler_params=pltpu.CompilerParams(
            collective_id=0, has_side_effects=True, vmem_limit_bytes=48 * 2**20
        ),
    )(padded(panel), padded(seeds[0]), inverses[0], coupling[0], place, factor, counts)
    ordered = proj[:, :dirs].reshape(R, NG, D, RG).transpose(0, 2, 1, 3).reshape(R, dirs)
    return flat(tangent)[None], flat(adjoint)[None], ordered


def solution(mesh):
    in_specs = (
        P("dir", None),
        P("seg", "dir", None),
        P("seg", "dir", None, None),
        P("seg", None, None, None),
        P(),
        P(),
        P(),
    )
    out_specs = (P("seg", "dir", None), P("seg", "dir", None), P("dir", None))
    return jax.shard_map(body, mesh=mesh, in_specs=in_specs, out_specs=out_specs, check_vma=False)
```

```python
import functools
import math

import jax
import jax.numpy as jnp
from jax import lax
from jax.experimental import pallas as pl
from jax.experimental.pallas import tpu as pltpu
from jax.sharding import PartitionSpec as P

MESH = pl.DeviceIdType.MESH
F32 = jnp.float32
BF16 = jnp.bfloat16

SEED, F1, F2, F3, TAN, HAND_F, HAND_G, G2, G3, G4, ADJ = range(11)
EXCHANGES = 11


def kernel(
    dims,
    panel_ref, seeds_ref, inv_ref, coup_ref, pat_ref, wts_ref, counts_ref,
    tangent_ref, adjoint_ref, proj_ref,
    land, f1s, f2s, f3s, tans, g2s, g3s, g4s, adjs, wf, wg, ubuf, obuf, pbuf, rp, qbuf, rq,
    send_sem, recv_sem, ps_sem, pr_sem, qs_sem, qr_sem,
):
    S, D, R, NG, nb, pb, B, K, scale = dims
    RG = R // NG
    N = D * pb
    rows = D * RG
    dirs = D * R
    s = lax.axis_index("seg")
    d = lax.axis_index("dir")
    tangent_first = s < lax.rem(1 - s + S, S)
    groups = range(NG)

    def partner(x):
        if D & (D - 1):
            return lax.rem(d + x, D)
        to, bit = d, 1
        while bit < D:
            if x & bit:
                to = to + bit * (1 - 2 * lax.rem(lax.div(d, bit), 2))
            bit *= 2
        return to

    def source(x):
        return lax.rem(d + D - x, D) if D & (D - 1) else partner(x)

    others = range(D - 1, 0, -1)

    barrier = pltpu.get_barrier_semaphore()
    total = S * D
    lin = s * D + d

    def greet(o, c):
        t = lax.rem(lin + o, total)
        pl.semaphore_signal(
            barrier, inc=1, device_id=(lax.div(t, D), lax.rem(t, D)), device_id_type=MESH
        )
        return c

    lax.fori_loop(1, total, greet, 0)

    spot = lax.broadcasted_iota(jnp.int32, (N, N), 1)

    def forward_matrix():
        for k in range(K):
            wf[:, k * N : (k + 1) * N] = jnp.where(
                pat_ref[:, k : k + 1] == spot, wts_ref[:, k : k + 1], 0.0
            ).astype(BF16)

    def adjoint_matrix():
        for k in range(K):
            wg[:, k * N : (k + 1) * N] = jnp.where(
                pat_ref[:, k : k + 1] == spot, wts_ref[:, k : k + 1], 0.0
            ).T.astype(BF16)

    @pl.when(tangent_first)
    def _():
        forward_matrix()

    obuf[...] = jnp.zeros_like(obuf)
    pl.semaphore_wait(barrier, total - 1)

    def copy(src, ex, g, seg, to, came_from):
        return pltpu.make_async_remote_copy(
            src_ref=src.at[g, to],
            dst_ref=land.at[ex, g, came_from],
            send_sem=send_sem.at[ex, g, to],
            recv_sem=recv_sem.at[ex, g, came_from],
            device_id=(seg, to),
            device_id_type=MESH,
        )

    def send_group(src, ex, g):
        for x in others:
            copy(src, ex, g, s, partner(x), d).start()
        land[ex, g, d] = src[g, d]

    def wait_group(src, ex, g):
        for x in others:
            j = source(x)
            copy(src, ex, g, s, j, j).wait_recv()

    def sent_group(src, ex):
        def one(o, c):
            for g in groups:
                copy(src, ex, g, s, lax.rem(d + o, D), d).wait_send()
            return c

        lax.fori_loop(1, D, one, 0)

    def send_on(src, ex, g, seg):
        for x in list(others) + [0]:
            copy(src, ex, g, seg, partner(x), d).start()

    def wait_on(src, ex, g, seg):
        for j in range(D):
            copy(src, ex, g, seg, j, j).wait_recv()

    def sent_on(src, ex, seg):
        def one(o, c):
            for g in groups:
                copy(src, ex, g, seg, o, d).wait_send()
            return c

        lax.fori_loop(0, D, one, 0)

    def give_back(arrived, ex, g, seg):
        return pltpu.make_async_remote_copy(
            src_ref=land.at[arrived, g],
            dst_ref=land.at[ex, g],
            send_sem=send_sem.at[ex, g, d],
            recv_sem=recv_sem.at[ex, g, d],
            device_id=(seg, d),
            device_id_type=MESH,
        )

    def couple(value, w_ref, contract):
        x = [value[:, r].reshape(N, B) for r in range(RG)]
        rhs = jnp.concatenate(
            [
                jnp.concatenate(
                    [
                        lax.dot_general(
                            v, coup_ref[k], (((1,), (contract,)), ((), ())),
                            preferred_element_type=F32,
                        ).astype(BF16)
                        for v in x
                    ],
                    axis=1,
                )
                for k in range(K)
            ],
            axis=0,
        )
        acc = jnp.dot(w_ref[...], rhs, preferred_element_type=F32)
        out = [x[r].astype(F32) + acc[:, r * B : (r + 1) * B] for r in range(RG)]
        return [v.astype(BF16).reshape(D, pb, B) for v in out]

    def put(ref, g, parts):
        for r in range(RG):
            ref[g, :, r] = parts[r]

    batch = max(n for n in range(1, 65) if nb % n == 0)

    def invert(value, contract):
        ubuf[...] = value.astype(F32).reshape(rows * pb, B)

        def step(i, c):
            for u in range(batch):
                at = pl.ds(i * batch + u, rows, stride=pb)
                obuf[at, :] = lax.dot_general(
                    ubuf[at, :].astype(BF16),
                    inv_ref[i * batch + u],
                    (((1,), (contract,)), ((), ())),
                    preferred_element_type=F32,
                )
            return c

        lax.fori_loop(0, nb // batch, step, 0)
        return obuf[...].astype(BF16).reshape(D, RG, pb, B)

    more = counts_ref[s] > 1

    def tangent_round():
        for g in groups:
            @pl.when(s > 0)
            def _():
                wait_on(tans, HAND_F, g, s)

            first = jnp.where(s > 0, land[HAND_F, g], panel_ref[g])
            put(f1s, g, couple(first, wf, 1))
            send_group(f1s, F1, g)

            @pl.when(s > 0)
            def _():
                give_back(HAND_F, TAN, g, s - 1).start()

        @pl.when(tangent_first)
        def _():
            adjoint_matrix()

        for g in groups:
            wait_group(f1s, F1, g)
            f2s[g] = invert(land[F1, g], 1)
            send_group(f2s, F2, g)

        @pl.when(s == 0)
        def _():
            send_group(seeds_ref, SEED, 0)

        for g in groups:
            wait_group(f2s, F2, g)
            put(f3s, g, couple(land[F2, g], wf, 1))
            send_group(f3s, F3, g)

        @pl.when(s == 0)
        def _():
            for g in groups[1:]:
                send_group(seeds_ref, SEED, g)

        for g in groups:
            wait_group(f3s, F3, g)
            tans[g] = jnp.where(more, invert(land[F3, g], 1), f2s[g])

            @pl.when(s < S - 1)
            def _():
                send_on(tans, HAND_F, g, lax.rem(s + 1, S))

            @pl.when(s == S - 1)
            def _():
                send_group(tans, TAN, g)

    def adjoint_round():
        for g in groups:
            wait_group(seeds_ref, SEED, g)

            @pl.when(s != 1)
            def _():
                wait_on(adjs, HAND_G, g, s)

            entry = jnp.where(
                s != 1,
                (land[SEED, g].astype(F32) + land[HAND_G, g].astype(F32)).astype(BF16),
                land[SEED, g],
            )
            g2s[g] = invert(entry, 0)
            send_group(g2s, G2, g)

            @pl.when(s != 1)
            def _():
                give_back(HAND_G, ADJ, g, lax.rem(s + 1, S)).start()

        @pl.when(jnp.logical_not(tangent_first))
        def _():
            adjoint_matrix()

        for g in groups:
            wait_group(g2s, G2, g)
            put(g3s, g, couple(land[G2, g], wg, 0))
            send_group(g3s, G3, g)

        @pl.when(jnp.logical_not(tangent_first))
        def _():
            forward_matrix()

        for g in groups:
            wait_group(g3s, G3, g)
            g4s[g] = invert(land[G3, g], 0)
            send_group(g4s, G4, g)
        for g in groups:
            wait_group(g4s, G4, g)
            last = couple(land[G4, g], wg, 0)
            put(adjs, g, [jnp.where(more, last[r], g3s[g, :, r]) for r in range(RG)])

            @pl.when(s != 2)
            def _():
                send_on(adjs, HAND_G, g, lax.rem(s + S - 1, S))

            @pl.when(s == 2)
            def _():
                send_group(adjs, ADJ, g)

    def turn(slot, c):
        now = (slot == 0) == tangent_first

        @pl.when(now)
        def _():
            tangent_round()

        @pl.when(jnp.logical_not(now))
        def _():
            adjoint_round()

        return c

    @pl.when(s != 0)
    def _():
        for g in groups:
            send_group(seeds_ref, SEED, g)

    lax.fori_loop(0, 2, turn, 0)

    for g in groups:
        for r in range(RG):
            adjoint_ref[:, g * RG + r] = adjs[g, :, r]

    pbuf[...] = jnp.zeros_like(pbuf)

    def gathered(buf, i):
        return jnp.concatenate(
            [buf[pl.ds(i * batch + u, rows, stride=pb), :].astype(BF16) for u in range(batch)],
            axis=1,
        )

    for g in groups:
        @pl.when(s == 2)
        def _():
            wait_group(adjs, ADJ, g)

        @pl.when(s != 2)
        def _():
            give_back(HAND_G, ADJ, g, s).wait_recv()

        ubuf[...] = land[ADJ, g].astype(F32).reshape(rows * pb, B)
        for h in groups:
            obuf[...] = tans[h].astype(F32).reshape(rows * pb, B)

            def gram(i, acc):
                return acc + lax.dot_general(
                    gathered(ubuf, i), gathered(obuf, i), (((1,), (1,)), ((), ())),
                    preferred_element_type=F32,
                )

            pbuf[g * rows : (g + 1) * rows, h * rows : (h + 1) * rows] = lax.fori_loop(
                0, nb // batch, gram, jnp.zeros((rows, rows), F32)
            )

    def pcopy(to, came_from):
        return pltpu.make_async_remote_copy(
            src_ref=pbuf, dst_ref=rp.at[came_from], send_sem=ps_sem.at[to],
            recv_sem=pr_sem.at[came_from], device_id=(s, to), device_id_type=MESH,
        )

    def qcopy(to, came_from):
        return pltpu.make_async_remote_copy(
            src_ref=qbuf, dst_ref=rq.at[came_from], send_sem=qs_sem.at[to],
            recv_sem=qr_sem.at[came_from], device_id=(to, d), device_id_type=MESH,
        )

    for x in others:
        pcopy(partner(x), d).start()
    rp[d] = pbuf[...]
    for x in others:
        j = source(x)
        pcopy(j, j).wait_recv()
    qbuf[...] = jnp.sum(rp[...], axis=0)
    for o in range(1, S):
        qcopy(lax.rem(s + o, S), s).start()
    rq[s] = qbuf[...]
    for g in groups:
        @pl.when(s == S - 1)
        def _():
            wait_group(tans, TAN, g)

        @pl.when(s < S - 1)
        def _():
            give_back(HAND_F, TAN, g, s).wait_recv()

        for r in range(RG):
            tangent_ref[:, g * RG + r] = land[TAN, g, :, r]
    for x in others:
        pcopy(partner(x), d).wait_send()
    for src, ex in (
        (seeds_ref, SEED), (f1s, F1), (f2s, F2), (f3s, F3),
        (g2s, G2), (g3s, G3), (g4s, G4),
    ):
        sent_group(src, ex)

    @pl.when(s < S - 1)
    def _():
        sent_on(tans, HAND_F, lax.rem(s + 1, S))

    @pl.when(s == S - 1)
    def _():
        sent_group(tans, TAN)

    @pl.when(s > 0)
    def _():
        for g in groups:
            give_back(HAND_F, TAN, g, s - 1).wait_send()

    @pl.when(s != 2)
    def _():
        sent_on(adjs, HAND_G, lax.rem(s + S - 1, S))

    @pl.when(s == 2)
    def _():
        sent_group(adjs, ADJ)

    @pl.when(s != 1)
    def _():
        for g in groups:
            give_back(HAND_G, ADJ, g, lax.rem(s + 1, S)).wait_send()

    for o in range(1, S):
        j = lax.rem(s + S - o, S)
        qcopy(j, j).wait_recv()
    pbuf[...] = jnp.sum(rq[...], axis=0) * scale
    for g in groups:
        proj_ref[g * RG : (g + 1) * RG, :] = pbuf[pl.ds(g * rows + d * RG, RG), :]
    for o in range(1, S):
        qcopy(lax.rem(s + o, S), s).wait_send()


def body(panel, seeds, inverses, coupling, weights, pattern, counts):
    NB, K = pattern.shape
    B = coupling.shape[-1]
    R = panel.shape[0]
    S, D = lax.axis_size("seg"), lax.axis_size("dir")
    nb = NB // D
    pb = -(-nb // 16) * 16
    N = D * pb
    NG = 2 if R % 2 == 0 else 1
    RG = R // NG
    rows, dirs = D * RG, D * R

    def padded(flat):
        cut = flat.reshape(NG, RG, D, nb, B).transpose(0, 2, 1, 3, 4)
        return jnp.pad(cut, ((0, 0),) * 3 + ((0, pb - nb), (0, 0)))

    def flat(cut):
        return cut[:, :, :nb].transpose(1, 0, 2, 3).reshape(R, NB * B)

    place = (pattern // nb) * pb + pattern % nb
    gap = ((0, 0), (0, pb - nb), (0, 0))
    place = jnp.pad(place.reshape(D, nb, K), gap, constant_values=-1).reshape(N, K)
    factor = jnp.pad(weights.reshape(D, nb, K), gap).reshape(N, K)

    dims = (S, D, R, NG, nb, pb, B, K, 1.0 / math.sqrt(NB * B * S))
    panel_buf = (NG, D, RG, pb, B)
    vm = pl.BlockSpec(memory_space=pltpu.VMEM)
    tangent, adjoint, proj = pl.pallas_call(
        functools.partial(kernel, dims),
        out_shape=(
            jax.ShapeDtypeStruct((D, R, pb, B), BF16),
            jax.ShapeDtypeStruct((D, R, pb, B), BF16),
            jax.ShapeDtypeStruct((R, 128), F32),
        ),
        in_specs=[vm] * 6 + [pl.BlockSpec(memory_space=pltpu.SMEM)],
        out_specs=(vm, vm, vm),
        scratch_shapes=[pltpu.VMEM((EXCHANGES,) + panel_buf, BF16)]
        + [pltpu.VMEM(panel_buf, BF16)] * 8
        + [
            pltpu.VMEM((N, K * N), BF16),
            pltpu.VMEM((N, K * N), BF16),
            pltpu.VMEM((rows * pb, B), F32),
            pltpu.VMEM((rows * pb, B), F32),
            pltpu.VMEM((dirs, 128), F32),
            pltpu.VMEM((D, dirs, 128), F32),
            pltpu.VMEM((dirs, 128), F32),
            pltpu.VMEM((S, dirs, 128), F32),
            pltpu.SemaphoreType.DMA((EXCHANGES, NG, D)),
            pltpu.SemaphoreType.DMA((EXCHANGES, NG, D)),
            pltpu.SemaphoreType.DMA((D,)),
            pltpu.SemaphoreType.DMA((D,)),
            pltpu.SemaphoreType.DMA((S,)),
            pltpu.SemaphoreType.DMA((S,)),
        ],
        compiler_params=pltpu.CompilerParams(
            collective_id=0, has_side_effects=True, vmem_limit_bytes=48 * 2**20
        ),
    )(padded(panel), padded(seeds[0]), inverses[0], coupling[0], place, factor, counts)
    ordered = proj[:, :dirs].reshape(R, NG, D, RG).transpose(0, 2, 1, 3).reshape(R, dirs)
    return flat(tangent)[None], flat(adjoint)[None], ordered


def solution(mesh):
    in_specs = (
        P("dir", None),
        P("seg", "dir", None),
        P("seg", "dir", None, None),
        P("seg", None, None, None),
        P(),
        P(),
        P(),
    )
    out_specs = (P("seg", "dir", None), P("seg", "dir", None), P("dir", None))
    return jax.shard_map(body, mesh=mesh, in_specs=in_specs, out_specs=out_specs, check_vma=False)
```
